32 devices in a mesh: tm: 8 (over z, y), space: 4 (over x, core).
Axes of the slice: x: 2, y: 2, z: 4, core: 2. Of those that a mesh axis runs over, the one named last changes fastest.
Arguments:
- initial_state: float32 [32, 16, 128], P('space'), may hold values from -6 to 6
- initial_guess: float32 [8, 32, 16, 128], P('tm', 'space'), may hold values from -6 to 6
- region: int32 [32, 16, 128], P('space'), may hold values from 0 to 7
- conductivity: float32 [8], replicated, may hold values from 0.036 to 0.046
- loss_table: float32 [8], replicated, may hold values from 0.0003 to 0.06
- heat_gain: float32 [32, 16, 128], P('space'), may hold values from 0.5 to 2
- levels: float32 [8], replicated, may hold values from -1 to 3
- plan: int32 [96], P('tm'), may hold values from 0 to 7
Outputs:
- c_points: float32 [8, 32, 16, 128], P('tm', 'space')
- defect: float32 [8, 32, 16, 128], P('tm', 'space')
The draws below stay inside these ranges and needn't reach their ends.
All inputs are finite; a program needn't handle non-finite values.
Results may differ from the reference program's by a relative error of at most 0.00009.
Values sent between devices are 32-bit elements; how exact they have to be, the bound alone decides.
A program may use at most 64 MiB of HBM per device.

```python
import math
import jax
import jax.numpy as jnp
from jax import lax

M = 12
SWEEPS = 2
R = 8
L = 8
SLICES = 8
STEPS = 96
NX = 32
NY = 16
NZ = 128


def with_ends(entries, key, least, top_value):
    extent = entries.shape
    place = [jax.random.randint(jax.random.fold_in(key, axis), (), 0, extent[axis]) for axis in range(len(extent))]
    entries = entries.at[tuple(place)].set(least)
    longest = extent.index(max(extent))
    place[longest] = (place[longest] + 1) % extent[longest]
    return entries.at[tuple(place)].set(top_value)


def block_levels(rng, shape, pieces, low, top_value):
    level = 1.0
    for axis_at, blocks in pieces:
        heights = jax.random.uniform(jax.random.fold_in(jax.random.fold_in(rng, 6), axis_at), (blocks,), jnp.float32, low / len(pieces), top_value / len(pieces))
        level = level * jnp.repeat(jnp.exp(heights), shape[axis_at] // blocks).reshape((-1,) + (1,) * (len(shape) - 1 - axis_at))
    return level


def centred(stream_key, dims, scale, reach, shards=(), kind=jnp.bfloat16):
    drawn = scale * jax.random.normal(stream_key, dims, jnp.float32)
    if shards:
        drawn = drawn * block_levels(stream_key, dims, shards, -0.22, 0.18)
    return jnp.clip(drawn, -reach, reach).astype(kind)


def setup_inputs(seed: int = 0) -> dict:
    keys = jax.random.split(jax.random.key(seed), 9)
    return {
        "initial_state": centred(keys[0], (NX, NY, NZ), 1.0, 6.0, ((0, 4),), jnp.float32),
        "initial_guess": centred(keys[1], (SLICES, NX, NY, NZ), 1.0, 6.0, ((0, 8), (1, 4)), jnp.float32),
        "region": with_ends(jax.random.randint(keys[2], (NX, NY, NZ), 0, R), jax.random.fold_in(keys[2], 1), 0, R - 1).astype(jnp.int32),
        "conductivity": jnp.clip(jax.random.uniform(keys[3], (R,), jnp.float32, 0.036, 0.046), 0.036, 0.046),
        "loss_table": jnp.clip(jnp.exp(jax.random.uniform(keys[4], (R,), jnp.float32, math.log(0.0003), math.log(0.06))), 0.0003, 0.06),
        "heat_gain": jnp.clip(0.5 + 1.5 * jax.random.uniform(keys[5], (NX, NY, NZ), jnp.float32) ** block_levels(keys[5], (NX, NY, NZ), ((0, 4),), -0.2, 0.2), 0.5, 2.0),
        "levels": jnp.clip(jax.random.uniform(keys[6], (L,), jnp.float32, -1.0, 3.0), -1.0, 3.0),
        "plan": with_ends(jax.random.randint(keys[7], (STEPS,), 0, L), jax.random.fold_in(keys[7], 1), 0, L - 1).astype(jnp.int32),
    }


source_gain = 0.1
in_plane = 8.0


def lookup(index_array, table):
    total = jnp.zeros(index_array.shape, jnp.float32)
    for entry in range(table.shape[0]):
        total = jnp.where(index_array == entry, table[entry], total)
    return total


def advance(widened, spread, loss_rate, heat_gain, current):
    padded = jnp.pad(widened, ((0, 0), (1, 1), (1, 1)))
    centre = padded[1:-1, 1:-1, 1:-1]
    along = padded[2:, 1:-1, 1:-1] + padded[:-2, 1:-1, 1:-1]
    across = padded[1:-1, 2:, 1:-1] + padded[1:-1, :-2, 1:-1]
    across = across + padded[1:-1, 1:-1, 2:] + padded[1:-1, 1:-1, :-2]
    flow = in_plane * (along - 2.0 * centre) + (across - 4.0 * centre)
    return centre + spread * flow - loss_rate * centre + (source_gain * current) * heat_gain


def reference(initial_state, initial_guess, region, conductivity, loss_table, heat_gain, levels, plan):
    spread = lookup(region, conductivity)
    loss_rate = lookup(region, loss_table)
    coarse_factor = 1.0 / (1.0 + M * loss_rate)
    currents = lookup(plan, levels).reshape(SLICES, M)

    def propagate(pair):
        field_now, current_row = pair
        for step_index in range(M):
            widened = jnp.pad(field_now, ((1, 1), (0, 0), (0, 0)))
            field_now = advance(widened, spread, loss_rate, heat_gain, current_row[step_index])
        return field_now

    def all_slices(fields):
        return lax.map(propagate, (fields, currents))

    def chain(carry_in, residue):
        carry_out = coarse_factor * carry_in + residue
        return carry_out, carry_out

    w_fields = initial_guess
    defect = jnp.zeros_like(initial_guess)
    for sweep_index in range(SWEEPS):
        slice_end = all_slices(w_fields)
        slice_start = jnp.concatenate([initial_state[None], slice_end[:-1]], axis=0)
        relaxed = all_slices(slice_start)
        defect = relaxed - slice_end
        _, correction = lax.scan(chain, jnp.zeros(initial_state.shape, jnp.float32), defect)
        w_fields = jnp.concatenate([initial_state[None], slice_end[:-1] + correction[:-1]], axis=0)
    return w_fields, defect
```

```python
import functools

import jax
import jax.numpy as jnp
from jax import lax
from jax.experimental import pallas as pl
from jax.experimental.pallas import tpu as pltpu
from jax.sharding import PartitionSpec as P

M = 12
MESH = pl.DeviceIdType.MESH

GROUP = 4


def halo_pieces(block):
    pieces, left, distance = [], M, 1
    while left > 0:
        pieces.append((distance, min(block, left)))
        left -= block
        distance += 1
    return pieces


def scan_distances(count):
    distances = []
    while not distances or distances[-1] * 2 < count:
        distances.append(distances[-1] * 2 if distances else 1)
    return [d for d in distances if d < count]


def kernel(
    times, spaces, block,
    w_ref, region_ref, gain_ref, init_ref, conduct_ref, loss_ref, levels_ref, plan_ref,
    out_ref, defect_ref,
    shift_src, shift_dst, region_buf, gain_buf, fields, other, diag_buf, spread_buf, factor_buf,
    sends, scan_src, scan_dst, kept,
    halo_send, halo_recv, shift_sems, scan_send, scan_recv,
):
    k, s = lax.axis_index("tm"), lax.axis_index("space")
    pieces = halo_pieces(block)
    distances = scan_distances(times)
    whole = block + 2 * M
    own = pl.ds(M, block)
    ny, nz = region_ref.shape[1:]

    barrier = pltpu.get_barrier_semaphore()
    expected = jnp.int32(0)
    for axis, mine, count, steps in (
        ("space", s, spaces, [d for d, _ in pieces]),
        ("tm", k, times, distances),
    ):
        for d in steps:
            for peer in (mine - d, mine + d):
                there = jnp.logical_and(peer >= 0, peer < count)
                expected = expected + there.astype(jnp.int32)

                @pl.when(there)
                def _(axis=axis, peer=peer):
                    pl.semaphore_signal(barrier, inc=1, device_id={axis: peer}, device_id_type=MESH)

    pl.semaphore_wait(barrier, expected)

    def halo_copies(number, source, target):
        out, into = [], []
        for at, (d, planes) in enumerate(pieces):
            low = M - (d - 1) * block - planes
            high = M + d * block
            for side, (first, place) in enumerate(((block - planes, low), (0, high))):
                to = s + d if side == 0 else s - d
                origin = s - d if side == 0 else s + d
                copy = pltpu.make_async_remote_copy(
                    src_ref=source.at[pl.ds(first, planes)],
                    dst_ref=target.at[pl.ds(place, planes)],
                    send_sem=halo_send.at[number, 2 * at + side],
                    recv_sem=halo_recv.at[number, 2 * at + side],
                    device_id={"space": to},
                    device_id_type=MESH,
                )
                out.append((jnp.logical_and(to >= 0, to < spaces), copy))
                into.append((jnp.logical_and(origin >= 0, origin < spaces), copy))
        return out, into

    def start(copies):
        for there, copy in copies:
            pl.when(there)(copy.start)

    def finish(copies):
        for there, copy in copies:
            pl.when(there)(copy.wait_recv)

    def drain(copies):
        for there, copy in copies:
            pl.when(there)(copy.wait_send)

    shift_src[pl.ds(0, block)] = w_ref[0]
    rows = lax.broadcasted_iota(jnp.int32, (ny, nz), 0)
    currents = jnp.zeros((ny, nz), jnp.float32)
    for step in range(M):
        currents = jnp.where(rows == step, 0.1 * levels_ref[plan_ref[step]], currents)
    shift_src[block] = currents
    has_before, has_after = k > 0, k < times - 1
    shift = pltpu.make_async_remote_copy(
        src_ref=shift_src, dst_ref=shift_dst, send_sem=shift_sems.at[0], recv_sem=shift_sems.at[1],
        device_id={"tm": k + 1}, device_id_type=MESH,
    )
    pl.when(has_after)(shift.start)

    region_out, region_in = halo_copies(0, region_ref, region_buf)
    gain_out, gain_in = halo_copies(1, gain_ref, gain_buf)
    start(region_out)
    start(gain_out)

    for d, planes in pieces:
        low = M - (d - 1) * block - planes
        high = M + d * block

        for there, place in ((s - d < 0, low), (s + d >= spaces, high)):
            @pl.when(there)
            def _(place=place, planes=planes):
                zero = jnp.zeros((planes, ny, nz), jnp.float32)
                region_buf[pl.ds(place, planes)] = jnp.full((planes, ny, nz), -1, jnp.int32)
                gain_buf[pl.ds(place, planes)] = zero
                for number in range(4):
                    fields[number, pl.ds(place, planes)] = zero

    region_buf[own] = region_ref[...]
    gain_buf[own] = gain_ref[...]

    @pl.when(k == 0)
    def _():
        shift_dst[...] = jnp.zeros_like(shift_dst)

    for at, d in enumerate(distances):
        @pl.when(k < d)
        def _(at=at):
            for scan in range(2):
                scan_dst[scan, at] = jnp.zeros((block, ny, nz), jnp.float32)

    pl.when(has_before)(shift.wait_recv)
    w_out, w_in = halo_copies(2, shift_dst, fields.at[0])
    start(w_out)
    fields[0, own] = shift_dst[pl.ds(0, block)]

    finish(region_in)

    def coefficients(p, _):
        index = region_buf[p]
        spread = jnp.zeros((ny, nz), jnp.float32)
        loss = jnp.zeros((ny, nz), jnp.float32)
        for entry in range(conduct_ref.shape[0]):
            here = index == entry
            spread = jnp.where(here, conduct_ref[entry], spread)
            loss = jnp.where(here, loss_ref[entry], loss)
        inside = jnp.where(index >= 0, 1.0, 0.0)
        spread_buf[p] = spread
        diag_buf[p] = inside - 20.0 * spread - loss
        factor_buf[p] = 1.0 / (1.0 + M * loss)
        return 0

    lax.fori_loop(0, whole, coefficients, 0)
    finish(gain_in)
    finish(w_in)

    lane = lax.broadcasted_iota(jnp.int32, (ny, nz), 1)
    first_lane, last_lane = lane == 0, lane == nz - 1
    first_row, last_row = rows == 0, rows == ny - 1

    def fine_step(source, target, margin, current):
        def plane(p, _):
            v = source[p]
            along = source[p - 1] + source[p + 1]
            across = jnp.where(first_lane, 0.0, pltpu.roll(v, 1, 1))
            across += jnp.where(last_lane, 0.0, pltpu.roll(v, nz - 1, 1))
            across += jnp.where(first_row, 0.0, pltpu.roll(v, 1, 0))
            across += jnp.where(last_row, 0.0, pltpu.roll(v, ny - 1, 0))
            new = diag_buf[p] * v + spread_buf[p] * (8.0 * along + across)
            if current is not None:
                new = new + current * gain_buf[p]
            target[p] = new
            return 0

        lax.fori_loop(margin, whole - margin, plane, 0, unroll=True)

    def propagate(field, sourced):
        for group in range(M // GROUP):
            margin = group * GROUP + 1

            def pair(at, _, group=group, margin=margin):
                step = group * GROUP + 2 * at
                for half, (source, target) in enumerate(((field, other), (other, field))):
                    current = None
                    if sourced:
                        row = shift_dst[block, pl.ds(step + half, 1), :]
                        current = jnp.broadcast_to(row, (ny, nz))
                    fine_step(source, target, margin, current)
                return 0

            lax.fori_loop(0, GROUP // 2, pair, 0)

    def exchange(number, value):
        sends[number - 3] = value
        out, into = halo_copies(number, sends.at[number - 3], fields.at[number - 2])
        start(out)
        fields[number - 2, own] = value
        finish(into)
        return out

    pending = []

    def scan(number, value, factor):
        power = factor
        for at, d in enumerate(distances):
            scan_src[number, at] = value
            copy = pltpu.make_async_remote_copy(
                src_ref=scan_src.at[number, at], dst_ref=scan_dst.at[number, at],
                send_sem=scan_send.at[number, at], recv_sem=scan_recv.at[number, at],
                device_id={"tm": k + d}, device_id_type=MESH,
            )
            pl.when(k + d < times)(copy.start)
            pl.when(k >= d)(copy.wait_recv)
            pending.append((k + d < times, copy))
            if at + 1 < len(distances):
                value = value + power * scan_dst[number, at]
                power = power * power

    def two_back(number, factor):
        square = factor * factor
        powers = [square]
        for _ in distances[2:]:
            powers.append(powers[-1] * powers[-1])
        total = jnp.zeros((block, ny, nz), jnp.float32)
        for at in reversed(range(1, len(distances))):
            total = scan_dst[number, at] + (powers[at - 1] * total if at + 1 < len(distances) else 0.0)
        return total

    propagate(fields.at[0], True)
    before = jnp.where(k == 0, init_ref[...], fields[0, own])
    kept[0] = before
    out_1 = exchange(3, before - w_ref[0])
    propagate(fields.at[1], False)

    factor = factor_buf[own]
    scan(0, fields[1, own], factor)
    carried = two_back(0, factor)
    out_2 = exchange(4, carried)
    propagate(fields.at[2], False)

    relaxed = fields[2, own]
    kept[0] = kept[0] + scan_dst[0, 0] + relaxed
    out_3 = exchange(5, relaxed - factor * sends[1])
    propagate(fields.at[3], False)
    defect = fields[3, own]
    defect_ref[0] = defect

    scan(1, defect, factor)
    corrected = kept[0] + scan_dst[1, 0] + factor * two_back(1, factor)
    out_ref[0] = jnp.where(k == 0, init_ref[...], corrected)

    pl.when(has_after)(shift.wait_send)
    for copies in (region_out, gain_out, w_out, out_1, out_2, out_3, pending):
        drain(copies)


def on_device(
    times, spaces,
    initial_state, initial_guess, region, conductivity, loss_table, heat_gain, levels, plan,
):
    block, ny, nz = region.shape
    whole = block + 2 * M
    pieces, laps = 2 * len(halo_pieces(block)), len(scan_distances(times))
    vmem = pl.BlockSpec(memory_space=pltpu.VMEM)
    smem = pl.BlockSpec(memory_space=pltpu.SMEM)
    f32 = jnp.float32
    return pl.pallas_call(
        functools.partial(kernel, times, spaces, block),
        out_shape=(jax.ShapeDtypeStruct((1, block, ny, nz), f32),) * 2,
        in_specs=[vmem] * 4 + [smem] * 4,
        out_specs=(vmem, vmem),
        scratch_shapes=[
            pltpu.VMEM((block + 1, ny, nz), f32),
            pltpu.VMEM((block + 1, ny, nz), f32),
            pltpu.VMEM((whole, ny, nz), jnp.int32),
            pltpu.VMEM((whole, ny, nz), f32),
            pltpu.VMEM((4, whole, ny, nz), f32),
            pltpu.VMEM((whole, ny, nz), f32),
            pltpu.VMEM((whole, ny, nz), f32),
            pltpu.VMEM((whole, ny, nz), f32),
            pltpu.VMEM((whole, ny, nz), f32),
            pltpu.VMEM((3, block, ny, nz), f32),
            pltpu.VMEM((2, laps, block, ny, nz), f32),
            pltpu.VMEM((2, laps, block, ny, nz), f32),
            pltpu.VMEM((1, block, ny, nz), f32),
            pltpu.SemaphoreType.DMA((6, pieces)),
            pltpu.SemaphoreType.DMA((6, pieces)),
            pltpu.SemaphoreType.DMA((2,)),
            pltpu.SemaphoreType.DMA((2, laps)),
            pltpu.SemaphoreType.DMA((2, laps)),
        ],
        compiler_params=pltpu.CompilerParams(
            collective_id=0, has_side_effects=True, vmem_limit_bytes=16 * 1024 * 1024
        ),
    )(initial_guess, region, heat_gain, initial_state, conductivity, loss_table, levels, plan)


def solution(mesh):
    placed = (
        P("space", None, None),
        P("tm", "space", None, None),
        P("space", None, None),
        P(),
        P(),
        P("space", None, None),
        P(),
        P("tm"),
    )
    return jax.shard_map(
        functools.partial(on_device, mesh.shape["tm"], mesh.shape["space"]),
        mesh=mesh,
        in_specs=placed,
        out_specs=(P("tm", "space", None, None), P("tm", "space", None, None)),
        check_vma=False,
    )
```

```python
import functools

import jax
import jax.numpy as jnp
from jax import lax
from jax.experimental import pallas as pl
from jax.experimental.pallas import tpu as pltpu
from jax.sharding import PartitionSpec as P

M = 12
MESH = pl.DeviceIdType.MESH

GROUP = 2


def halo_pieces(block):
    pieces, left, distance = [], M, 1
    while left > 0:
        pieces.append((distance, min(block, left)))
        left -= block
        distance += 1
    return pieces


def scan_distances(count):
    distances = []
    while not distances or distances[-1] * 2 < count:
        distances.append(distances[-1] * 2 if distances else 1)
    return [d for d in distances if d < count]


def kernel(
    times, spaces, block,
    w_ref, region_ref, gain_ref, init_ref, conduct_hbm, loss_hbm, levels_hbm, plan_hbm,
    out_ref, defect_ref,
    w_buf, init_buf, conduct_ref, loss_ref, levels_ref, plan_ref,
    current_src, current_dst, shift_dst, region_buf, gain_buf, fields, other, diag_buf, spread_buf, factor_buf,
    sends, scan_src, scan_dst, kept,
    halo_send, halo_recv, shift_sems, scan_send, scan_recv, load_sems,
):
    k, s = lax.axis_index("tm"), lax.axis_index("space")
    pieces = halo_pieces(block)
    distances = scan_distances(times)
    whole = block + 2 * M
    own = pl.ds(M, block)
    ny, nz = region_ref.shape[1:]

    loads = [
        pltpu.make_async_copy(source, target, load_sems.at[at])
        for at, (source, target) in enumerate((
            (levels_hbm, levels_ref), (plan_hbm, plan_ref), (conduct_hbm, conduct_ref),
            (loss_hbm, loss_ref), (region_ref, region_buf.at[own]), (gain_ref, gain_buf.at[own]),
            (w_ref.at[0], w_buf), (init_ref, init_buf),
        ))
    ]
    for load in loads:
        load.start()

    barrier = pltpu.get_barrier_semaphore()
    expected = jnp.int32(0)
    for axis, mine, count, steps in (
        ("space", s, spaces, [d for d, _ in pieces]),
        ("tm", k, times, distances),
    ):
        for d in steps:
            for peer in (mine - d, mine + d):
                there = jnp.logical_and(peer >= 0, peer < count)
                expected = expected + there.astype(jnp.int32)

                @pl.when(there)
                def _(axis=axis, peer=peer):
                    pl.semaphore_signal(barrier, inc=1, device_id={axis: peer}, device_id_type=MESH)

    pl.semaphore_wait(barrier, expected)

    def halo_copies(number, source, target):
        out, into = [], []
        for at, (d, planes) in enumerate(pieces):
            low = M - (d - 1) * block - planes
            high = M + d * block
            for side, (first, place) in enumerate(((block - planes, low), (0, high))):
                to = s + d if side == 0 else s - d
                origin = s - d if side == 0 else s + d
                copy = pltpu.make_async_remote_copy(
                    src_ref=source.at[pl.ds(first, planes)],
                    dst_ref=target.at[pl.ds(place, planes)],
                    send_sem=halo_send.at[number, 2 * at + side],
                    recv_sem=halo_recv.at[number, 2 * at + side],
                    device_id={"space": to},
                    device_id_type=MESH,
                )
                out.append((jnp.logical_and(to >= 0, to < spaces), copy))
                into.append((jnp.logical_and(origin >= 0, origin < spaces), copy))
        return out, into

    def start(copies):
        for there, copy in copies:
            pl.when(there)(copy.start)

    def finish(copies):
        for there, copy in copies:
            pl.when(there)(copy.wait_recv)

    def drain(copies):
        for there, copy in copies:
            pl.when(there)(copy.wait_send)

    has_before, has_after = k > 0, k < times - 1
    shift = pltpu.make_async_remote_copy(
        src_ref=w_ref.at[0], dst_ref=shift_dst, send_sem=shift_sems.at[0], recv_sem=shift_sems.at[1],
        device_id={"tm": k + 1}, device_id_type=MESH,
    )
    pl.when(has_after)(shift.start)

    region_out, region_in = halo_copies(0, region_ref, region_buf)
    gain_out, gain_in = halo_copies(1, gain_ref, gain_buf)
    start(region_out)
    start(gain_out)

    for load in loads[:2]:
        load.wait()
    rows = lax.broadcasted_iota(jnp.int32, (ny, nz), 0)
    currents = jnp.zeros((ny, nz), jnp.float32)
    for step in range(M):
        currents = jnp.where(rows == step, 0.1 * levels_ref[plan_ref[step]], currents)
    current_src[...] = currents
    current_shift = pltpu.make_async_remote_copy(
        src_ref=current_src, dst_ref=current_dst, send_sem=shift_sems.at[2], recv_sem=shift_sems.at[3],
        device_id={"tm": k + 1}, device_id_type=MESH,
    )
    pl.when(has_after)(current_shift.start)

    for d, planes in pieces:
        low = M - (d - 1) * block - planes
        high = M + d * block

        for there, place in ((s - d < 0, low), (s + d >= spaces, high)):
            @pl.when(there)
            def _(place=place, planes=planes):
                zero = jnp.zeros((planes, ny, nz), jnp.float32)
                region_buf[pl.ds(place, planes)] = jnp.full((planes, ny, nz), -1, jnp.int32)
                gain_buf[pl.ds(place, planes)] = zero
                for number in range(4):
                    fields[number, pl.ds(place, planes)] = zero

    @pl.when(k == 0)
    def _():
        shift_dst[...] = jnp.zeros_like(shift_dst)
        current_dst[...] = jnp.zeros_like(current_dst)

    for at, d in enumerate(distances):
        @pl.when(k < d)
        def _(at=at):
            for scan in range(2):
                scan_dst[scan, at] = jnp.zeros((block, ny, nz), jnp.float32)

    pl.when(has_before)(shift.wait_recv)
    w_out, w_in = halo_copies(2, shift_dst, fields.at[0])
    start(w_out)
    fields[0, own] = shift_dst[...]
    for load in loads[2:]:
        load.wait()

    finish(region_in)

    def coefficients(p, _):
        index = region_buf[p]
        spread = jnp.zeros((ny, nz), jnp.float32)
        loss = jnp.zeros((ny, nz), jnp.float32)
        for entry in range(conduct_ref.shape[0]):
            here = index == entry
            spread = jnp.where(here, conduct_ref[entry], spread)
            loss = jnp.where(here, loss_ref[entry], loss)
        inside = jnp.where(index >= 0, 1.0, 0.0)
        spread_buf[p] = spread
        diag_buf[p] = inside - 20.0 * spread - loss
        factor_buf[p] = 1.0 / (1.0 + M * loss)
        return 0

    lax.fori_loop(0, whole, coefficients, 0)
    finish(gain_in)
    pl.when(has_before)(current_shift.wait_recv)
    finish(w_in)

    lane = lax.broadcasted_iota(jnp.int32, (ny, nz), 1)
    first_lane, last_lane = lane == 0, lane == nz - 1
    first_row, last_row = rows == 0, rows == ny - 1

    def fine_step(source, target, margin, current):
        def plane(p, _):
            v = source[p]
            along = source[p - 1] + source[p + 1]
            across = jnp.where(first_lane, 0.0, pltpu.roll(v, 1, 1))
            across += jnp.where(last_lane, 0.0, pltpu.roll(v, nz - 1, 1))
            across += jnp.where(first_row, 0.0, pltpu.roll(v, 1, 0))
            across += jnp.where(last_row, 0.0, pltpu.roll(v, ny - 1, 0))
            new = diag_buf[p] * v + spread_buf[p] * (8.0 * along + across)
            if current is not None:
                new = new + current * gain_buf[p]
            target[p] = new
            return 0

        lax.fori_loop(margin, whole - margin, plane, 0, unroll=True)

    def propagate(field, sourced):
        for group in range(M // GROUP):
            margin = group * GROUP + 1

            def pair(at, _, group=group, margin=margin):
                step = group * GROUP + 2 * at
                for half, (source, target) in enumerate(((field, other), (other, field))):
                    current = None
                    if sourced:
                        row = current_dst[pl.ds(step + half, 1), :]
                        current = jnp.broadcast_to(row, (ny, nz))
                    fine_step(source, target, margin, current)
                return 0

            lax.fori_loop(0, GROUP // 2, pair, 0)

    def exchange(number, value):
        sends[number - 3] = value
        out, into = halo_copies(number, sends.at[number - 3], fields.at[number - 2])
        start(out)
        fields[number - 2, own] = value
        finish(into)
        return out

    pending = []

    def scan(number, value, factor):
        power = factor
        for at, d in enumerate(distances):
            scan_src[number, at] = value
            copy = pltpu.make_async_remote_copy(
                src_ref=scan_src.at[number, at], dst_ref=scan_dst.at[number, at],
                send_sem=scan_send.at[number, at], recv_sem=scan_recv.at[number, at],
                device_id={"tm": k + d}, device_id_type=MESH,
            )
            pl.when(k + d < times)(copy.start)
            pl.when(k >= d)(copy.wait_recv)
            pending.append((k + d < times, copy))
            if at + 1 < len(distances):
                value = value + power * scan_dst[number, at]
                power = power * power

    def two_back(number, factor):
        square = factor * factor
        powers = [square]
        for _ in distances[2:]:
            powers.append(powers[-1] * powers[-1])
        total = jnp.zeros((block, ny, nz), jnp.float32)
        for at in reversed(range(1, len(distances))):
            total = scan_dst[number, at] + (powers[at - 1] * total if at + 1 < len(distances) else 0.0)
        return total

    propagate(fields.at[0], True)
    before = jnp.where(k == 0, init_buf[...], fields[0, own])
    kept[0] = before
    out_1 = exchange(3, before - w_buf[...])
    propagate(fields.at[1], False)

    factor = factor_buf[own]
    scan(0, fields[1, own], factor)
    carried = two_back(0, factor)
    out_2 = exchange(4, carried)
    propagate(fields.at[2], False)

    relaxed = fields[2, own]
    kept[0] = kept[0] + scan_dst[0, 0] + relaxed
    out_3 = exchange(5, relaxed - factor * sends[1])
    propagate(fields.at[3], False)
    defect = fields[3, own]
    defect_ref[0] = defect

    scan(1, defect, factor)
    corrected = kept[0] + scan_dst[1, 0] + factor * two_back(1, factor)
    out_ref[0] = jnp.where(k == 0, init_buf[...], corrected)

    pl.when(has_after)(shift.wait_send)
    pl.when(has_after)(current_shift.wait_send)
    for copies in (region_out, gain_out, w_out, out_1, out_2, out_3, pending):
        drain(copies)


def on_device(
    times, spaces,
    initial_state, initial_guess, region, conductivity, loss_table, heat_gain, levels, plan,
):
    block, ny, nz = region.shape
    whole = block + 2 * M
    pieces, laps = 2 * len(halo_pieces(block)), len(scan_distances(times))
    vmem = pl.BlockSpec(memory_space=pltpu.VMEM)
    hbm = pl.BlockSpec(memory_space=pltpu.HBM)
    f32 = jnp.float32
    return pl.pallas_call(
        functools.partial(kernel, times, spaces, block),
        out_shape=(jax.ShapeDtypeStruct((1, block, ny, nz), f32),) * 2,
        in_specs=[hbm] * 8,
        out_specs=(vmem, vmem),
        scratch_shapes=[
            pltpu.VMEM((block, ny, nz), f32),
            pltpu.VMEM((block, ny, nz), f32),
            pltpu.SMEM(conductivity.shape, f32),
            pltpu.SMEM(loss_table.shape, f32),
            pltpu.SMEM(levels.shape, f32),
            pltpu.SMEM(plan.shape, plan.dtype),
            pltpu.VMEM((ny, nz), f32),
            pltpu.VMEM((ny, nz), f32),
            pltpu.VMEM((block, ny, nz), f32),
            pltpu.VMEM((whole, ny, nz), jnp.int32),
            pltpu.VMEM((whole, ny, nz), f32),
            pltpu.VMEM((4, whole, ny, nz), f32),
            pltpu.VMEM((whole, ny, nz), f32),
            pltpu.VMEM((whole, ny, nz), f32),
            pltpu.VMEM((whole, ny, nz), f32),
            pltpu.VMEM((whole, ny, nz), f32),
            pltpu.VMEM((3, block, ny, nz), f32),
            pltpu.VMEM((2, laps, block, ny, nz), f32),
            pltpu.VMEM((2, laps, block, ny, nz), f32),
            pltpu.VMEM((1, block, ny, nz), f32),
            pltpu.SemaphoreType.DMA((6, pieces)),
            pltpu.SemaphoreType.DMA((6, pieces)),
            pltpu.SemaphoreType.DMA((4,)),
            pltpu.SemaphoreType.DMA((2, laps)),
            pltpu.SemaphoreType.DMA((2, laps)),
            pltpu.SemaphoreType.DMA((8,)),
        ],
        compiler_params=pltpu.CompilerParams(
            collective_id=0, has_side_effects=True, vmem_limit_bytes=64 * 1024 * 1024
        ),
    )(initial_guess, region, heat_gain, initial_state, conductivity, loss_table, levels, plan)


def solution(mesh):
    placed = (
        P("space", None, None),
        P("tm", "space", None, None),
        P("space", None, None),
        P(),
        P(),
        P("space", None, None),
        P(),
        P("tm"),
    )
    return jax.shard_map(
        functools.partial(on_device, mesh.shape["tm"], mesh.shape["space"]),
        mesh=mesh,
        in_specs=placed,
        out_specs=(P("tm", "space", None, None), P("tm", "space", None, None)),
        check_vma=False,
    )
```

```python
import functools

import jax
import jax.numpy as jnp
from jax import lax
from jax.experimental import pallas as pl
from jax.experimental.pallas import tpu as pltpu
from jax.sharding import PartitionSpec as P

M = 12
MESH = pl.DeviceIdType.MESH

GROUP = 2


def halo_pieces(block):
    pieces, left, distance = [], M, 1
    while left > 0:
        pieces.append((distance, min(block, left)))
        left -= block
        distance += 1
    return pieces


def scan_distances(count):
    distances = []
    while not distances or distances[-1] * 2 < count:
        distances.append(distances[-1] * 2 if distances else 1)
    return [d for d in distances if d < count]


def kernel(
    times, spaces, block,
    w_ref, region_ref, gain_ref, init_ref, conduct_hbm, loss_hbm, levels_hbm, plan_hbm,
    both_ref,
    w_buf, init_buf, conduct_ref, loss_ref, levels_ref, plan_ref,
    current_src, current_dst, shift_dst, region_buf, gain_buf, fields, other, diag_buf, spread_buf, factor_buf,
    sends, scan_src, scan_dst, kept,
    halo_send, halo_recv, shift_sems, scan_send, scan_recv, load_sems,
):
    k, s = lax.axis_index("tm"), lax.axis_index("space")
    pieces = halo_pieces(block)
    distances = scan_distances(times)
    whole = block + 2 * M
    own = pl.ds(M, block)
    ny, nz = region_ref.shape[1:]

    loads = [
        pltpu.make_async_copy(source, target, load_sems.at[at])
        for at, (source, target) in enumerate((
            (levels_hbm, levels_ref), (plan_hbm, plan_ref), (conduct_hbm, conduct_ref),
            (loss_hbm, loss_ref), (region_ref, region_buf.at[own]), (gain_ref, gain_buf.at[own]),
            (w_ref.at[0], w_buf), (init_ref, init_buf),
        ))
    ]
    for load in loads:
        load.start()

    barrier = pltpu.get_barrier_semaphore()
    expected = jnp.int32(0)
    for axis, mine, count, steps in (
        ("space", s, spaces, [d for d, _ in pieces]),
        ("tm", k, times, distances),
    ):
        for d in steps:
            for peer in (mine - d, mine + d):
                there = jnp.logical_and(peer >= 0, peer < count)
                expected = expected + there.astype(jnp.int32)

                @pl.when(there)
                def _(axis=axis, peer=peer):
                    pl.semaphore_signal(barrier, inc=1, device_id={axis: peer}, device_id_type=MESH)

    pl.semaphore_wait(barrier, expected)

    def halo_copies(number, source, target):
        out, into = [], []
        for at, (d, planes) in enumerate(pieces):
            low = M - (d - 1) * block - planes
            high = M + d * block
            for side, (first, place) in enumerate(((block - planes, low), (0, high))):
                to = s + d if side == 0 else s - d
                origin = s - d if side == 0 else s + d
                copy = pltpu.make_async_remote_copy(
                    src_ref=source.at[pl.ds(first, planes)],
                    dst_ref=target.at[pl.ds(place, planes)],
                    send_sem=halo_send.at[number, 2 * at + side],
                    recv_sem=halo_recv.at[number, 2 * at + side],
                    device_id={"space": to},
                    device_id_type=MESH,
                )
                out.append((jnp.logical_and(to >= 0, to < spaces), copy))
                into.append((jnp.logical_and(origin >= 0, origin < spaces), copy))
        return out, into

    def start(copies):
        for there, copy in copies:
            pl.when(there)(copy.start)

    def finish(copies):
        for there, copy in copies:
            pl.when(there)(copy.wait_recv)

    def drain(copies):
        for there, copy in copies:
            pl.when(there)(copy.wait_send)

    has_before, has_after = k > 0, k < times - 1
    shift = pltpu.make_async_remote_copy(
        src_ref=w_ref.at[0], dst_ref=shift_dst, send_sem=shift_sems.at[0], recv_sem=shift_sems.at[1],
        device_id={"tm": k + 1}, device_id_type=MESH,
    )
    pl.when(has_after)(shift.start)

    region_out, region_in = halo_copies(0, region_ref, region_buf)
    gain_out, gain_in = halo_copies(1, gain_ref, gain_buf)
    start(region_out)
    start(gain_out)

    for load in loads[:2]:
        load.wait()
    rows = lax.broadcasted_iota(jnp.int32, (ny, nz), 0)
    currents = jnp.zeros((ny, nz), jnp.float32)
    for step in range(M):
        currents = jnp.where(rows == step, 0.1 * levels_ref[plan_ref[step]], currents)
    current_src[...] = currents
    current_shift = pltpu.make_async_remote_copy(
        src_ref=current_src, dst_ref=current_dst, send_sem=shift_sems.at[2], recv_sem=shift_sems.at[3],
        device_id={"tm": k + 1}, device_id_type=MESH,
    )
    pl.when(has_after)(current_shift.start)

    for d, planes in pieces:
        low = M - (d - 1) * block - planes
        high = M + d * block

        for there, place in ((s - d < 0, low), (s + d >= spaces, high)):
            @pl.when(there)
            def _(place=place, planes=planes):
                zero = jnp.zeros((planes, ny, nz), jnp.float32)
                region_buf[pl.ds(place, planes)] = jnp.full((planes, ny, nz), -1, jnp.int32)
                gain_buf[pl.ds(place, planes)] = zero
                for number in range(4):
                    fields[number, pl.ds(place, planes)] = zero

    @pl.when(k == 0)
    def _():
        shift_dst[...] = jnp.zeros_like(shift_dst)
        current_dst[...] = jnp.zeros_like(current_dst)

    for at, d in enumerate(distances):
        @pl.when(k < d)
        def _(at=at):
            for scan in range(2):
                scan_dst[scan, at] = jnp.zeros((block, ny, nz), jnp.float32)

    pl.when(has_before)(shift.wait_recv)
    w_out, w_in = halo_copies(2, shift_dst, fields.at[0])
    start(w_out)
    fields[0, own] = shift_dst[...]
    for load in loads[2:]:
        load.wait()

    finish(region_in)

    def coefficients(p, _):
        index = region_buf[p]
        spread = jnp.zeros((ny, nz), jnp.float32)
        loss = jnp.zeros((ny, nz), jnp.float32)
        for entry in range(conduct_ref.shape[0]):
            here = index == entry
            spread = jnp.where(here, conduct_ref[entry], spread)
            loss = jnp.where(here, loss_ref[entry], loss)
        inside = jnp.where(index >= 0, 1.0, 0.0)
        spread_buf[p] = spread
        diag_buf[p] = inside - 20.0 * spread - loss
        factor_buf[p] = 1.0 / (1.0 + M * loss)
        return 0

    lax.fori_loop(0, whole, coefficients, 0)
    finish(gain_in)
    pl.when(has_before)(current_shift.wait_recv)
    finish(w_in)

    lane = lax.broadcasted_iota(jnp.int32, (ny, nz), 1)
    first_lane, last_lane = lane == 0, lane == nz - 1
    first_row, last_row = rows == 0, rows == ny - 1

    def fine_step(source, target, margin, current):
        def plane(p, _):
            v = source[p]
            along = source[p - 1] + source[p + 1]
            across = jnp.where(first_lane, 0.0, pltpu.roll(v, 1, 1))
            across += jnp.where(last_lane, 0.0, pltpu.roll(v, nz - 1, 1))
            across += jnp.where(first_row, 0.0, pltpu.roll(v, 1, 0))
            across += jnp.where(last_row, 0.0, pltpu.roll(v, ny - 1, 0))
            new = diag_buf[p] * v + spread_buf[p] * (8.0 * along + across)
            if current is not None:
                new = new + current * gain_buf[p]
            target[p] = new
            return 0

        lax.fori_loop(margin, whole - margin, plane, 0, unroll=True)

    def propagate(field, sourced):
        for group in range(M // GROUP):
            margin = group * GROUP + 1

            def pair(at, _, group=group, margin=margin):
                step = group * GROUP + 2 * at
                for half, (source, target) in enumerate(((field, other), (other, field))):
                    current = None
                    if sourced:
                        row = current_dst[pl.ds(step + half, 1), :]
                        current = jnp.broadcast_to(row, (ny, nz))
                    fine_step(source, target, margin, current)
                return 0

            lax.fori_loop(0, GROUP // 2, pair, 0)

    def exchange(number, value):
        sends[number - 3] = value
        out, into = halo_copies(number, sends.at[number - 3], fields.at[number - 2])
        start(out)
        fields[number - 2, own] = value
        finish(into)
        return out

    pending = []

    def scan(number, value, factor):
        power = factor
        for at, d in enumerate(distances):
            scan_src[number, at] = value
            copy = pltpu.make_async_remote_copy(
                src_ref=scan_src.at[number, at], dst_ref=scan_dst.at[number, at],
                send_sem=scan_send.at[number, at], recv_sem=scan_recv.at[number, at],
                device_id={"tm": k + d}, device_id_type=MESH,
            )
            pl.when(k + d < times)(copy.start)
            pl.when(k >= d)(copy.wait_recv)
            pending.append((k + d < times, copy))
            if at + 1 < len(distances):
                value = value + power * scan_dst[number, at]
                power = power * power

    def two_back(number, factor):
        square = factor * factor
        powers = [square]
        for _ in distances[2:]:
            powers.append(powers[-1] * powers[-1])
        total = jnp.zeros((block, ny, nz), jnp.float32)
        for at in reversed(range(1, len(distances))):
            total = scan_dst[number, at] + (powers[at - 1] * total if at + 1 < len(distances) else 0.0)
        return total

    propagate(fields.at[0], True)
    before = jnp.where(k == 0, init_buf[...], fields[0, own])
    kept[0] = before
    out_1 = exchange(3, before - w_buf[...])
    propagate(fields.at[1], False)

    factor = factor_buf[own]
    scan(0, fields[1, own], factor)
    carried = two_back(0, factor)
    out_2 = exchange(4, carried)
    propagate(fields.at[2], False)

    relaxed = fields[2, own]
    kept[0] = kept[0] + scan_dst[0, 0] + relaxed
    out_3 = exchange(5, relaxed - factor * sends[1])
    propagate(fields.at[3], False)
    defect = fields[3, own]
    both_ref[1] = defect

    scan(1, defect, factor)
    corrected = kept[0] + scan_dst[1, 0] + factor * two_back(1, factor)
    both_ref[0] = jnp.where(k == 0, init_buf[...], corrected)

    pl.when(has_after)(shift.wait_send)
    pl.when(has_after)(current_shift.wait_send)
    for copies in (region_out, gain_out, w_out, out_1, out_2, out_3, pending):
        drain(copies)


def on_device(
    times, spaces,
    initial_state, initial_guess, region, conductivity, loss_table, heat_gain, levels, plan,
):
    block, ny, nz = region.shape
    whole = block + 2 * M
    pieces, laps = 2 * len(halo_pieces(block)), len(scan_distances(times))
    vmem = pl.BlockSpec(memory_space=pltpu.VMEM)
    hbm = pl.BlockSpec(memory_space=pltpu.HBM)
    f32 = jnp.float32
    both = pl.pallas_call(
        functools.partial(kernel, times, spaces, block),
        out_shape=jax.ShapeDtypeStruct((2, block, ny, nz), f32),
        in_specs=[hbm] * 8,
        out_specs=vmem,
        scratch_shapes=[
            pltpu.VMEM((block, ny, nz), f32),
            pltpu.VMEM((block, ny, nz), f32),
            pltpu.SMEM(conductivity.shape, f32),
            pltpu.SMEM(loss_table.shape, f32),
            pltpu.SMEM(levels.shape, f32),
            pltpu.SMEM(plan.shape, plan.dtype),
            pltpu.VMEM((ny, nz), f32),
            pltpu.VMEM((ny, nz), f32),
            pltpu.VMEM((block, ny, nz), f32),
            pltpu.VMEM((whole, ny, nz), jnp.int32),
            pltpu.VMEM((whole, ny, nz), f32),
            pltpu.VMEM((4, whole, ny, nz), f32),
            pltpu.VMEM((whole, ny, nz), f32),
            pltpu.VMEM((whole, ny, nz), f32),
            pltpu.VMEM((whole, ny, nz), f32),
            pltpu.VMEM((whole, ny, nz), f32),
            pltpu.VMEM((3, block, ny, nz), f32),
            pltpu.VMEM((2, laps, block, ny, nz), f32),
            pltpu.VMEM((2, laps, block, ny, nz), f32),
            pltpu.VMEM((1, block, ny, nz), f32),
            pltpu.SemaphoreType.DMA((6, pieces)),
            pltpu.SemaphoreType.DMA((6, pieces)),
            pltpu.SemaphoreType.DMA((4,)),
            pltpu.SemaphoreType.DMA((2, laps)),
            pltpu.SemaphoreType.DMA((2, laps)),
            pltpu.SemaphoreType.DMA((8,)),
        ],
        compiler_params=pltpu.CompilerParams(
            collective_id=0, has_side_effects=True, vmem_limit_bytes=64 * 1024 * 1024
        ),
    )(initial_guess, region, heat_gain, initial_state, conductivity, loss_table, levels, plan)
    return both[:1], both[1:]


def solution(mesh):
    placed = (
        P("space", None, None),
        P("tm", "space", None, None),
        P("space", None, None),
        P(),
        P(),
        P("space", None, None),
        P(),
        P("tm"),
    )
    return jax.shard_map(
        functools.partial(on_device, mesh.shape["tm"], mesh.shape["space"]),
        mesh=mesh,
        in_specs=placed,
        out_specs=(P("tm", "space", None, None), P("tm", "space", None, None)),
        check_vma=False,
    )
```
